32 devices in a mesh: row: 2 (over x), blk: 16 (over z, y, core).
Axes of the slice: x: 2, y: 2, z: 4, core: 2. Of those that a mesh axis runs over, the one named last changes fastest.
Arguments:
- matrix: float32 [4096, 2048], P('row', 'blk'), may hold values from -72 to 72, as said below
- prior: float32 [2048, 2048], P('row', 'blk'), may hold values from -6 to 6
Outputs:
- turned: float32 [4096, 2048], P('row', 'blk')
- transform: float32 [2048, 2048], P('row', 'blk')
- off_ratio: float32 [8], replicated
The draws below stay inside these ranges and needn't reach their ends.
Inputs may be any that keep to these rules, and one draw needn't show every extreme that they name: `matrix`: every column is nonzero.
All inputs are finite; a program needn't handle non-finite values.
Results may differ from the reference program's by a relative error of at most 0.0003.
Values sent between devices are 32-bit elements; how exact they have to be, the bound alone decides.
A program may use at most 64 MiB of HBM per device.

```python
import jax
import jax.numpy as jnp
from jax import lax

ROUNDS = 8
NS_STEPS = 8
ROWS = 4096
COLS = 2048
N_BLK = 16


def draw_matrix(key, part):
    keys = jax.random.split(key, 5)
    noise = jnp.clip(jax.random.normal(keys[0], (ROWS, COLS), jnp.float32), -6.0, 6.0)
    strength = 0.6
    common_rows = jnp.clip(jax.random.normal(keys[1], (ROWS, 1), jnp.float32), -6.0, 6.0)
    common_cols = jax.random.uniform(keys[2], (1, COLS), jnp.float32, -1.0, 1.0)
    row_scale = jnp.exp(jax.random.uniform(keys[3], (ROWS, 1), jnp.float32, jnp.log(0.3), jnp.log(3.0)))
    position = jnp.arange(COLS, dtype=jnp.float32)[None, :] / COLS
    col_scale = jnp.exp(jax.random.uniform(keys[4], (1, COLS), jnp.float32, jnp.log(0.5), jnp.log(2.0))) * jnp.exp(-1.2 * position)
    return row_scale * col_scale * (noise + strength * common_rows * common_cols)


def block_scale(stream_key, extent, pieces, least, top_value):
    def one(dim, parts):
        draws = jax.random.uniform(jax.random.fold_in(jax.random.fold_in(stream_key, 6), dim), (parts,), jnp.float32, least / len(pieces), top_value / len(pieces))
        return jnp.repeat(jnp.exp(draws), extent[dim] // parts).reshape((-1,) + (1,) * (len(extent) - dim - 1))

    gain = one(*pieces[0])
    for cut in pieces[1:]:
        gain = gain * one(*cut)
    return gain


def gaussian(own_key, extent, spread, limit, cuts=(), kind=jnp.bfloat16):
    gain = block_scale(own_key, extent, cuts, -0.22, 0.18) if cuts else 1.0
    values = jax.random.normal(own_key, extent, jnp.float32) * spread * gain
    return jnp.minimum(jnp.maximum(values, -limit), limit).astype(kind)


def setup_inputs(seed: int = 0) -> dict:
    arg_keys = jax.random.split(jax.random.key(seed), 3)
    return {
        "matrix": draw_matrix(jax.random.fold_in(arg_keys[2], 71), 0),
        "prior": gaussian(arg_keys[1], (COLS, COLS), 1.0, 6.0, ((0, 2), (1, 16)), jnp.float32),
    }


HIGH = lax.Precision.HIGHEST

def rotation(gram_sum):
    pair_width = gram_sum.shape[0]
    diag_vals = jnp.diagonal(gram_sum)
    weights = jnp.arange(pair_width, dtype=jnp.float32) / pair_width
    mean_diag = jnp.mean(diag_vals)
    skew_part = gram_sum * (weights[None, :] - weights[:, None]) / mean_diag
    factor = lax.rsqrt(1.0 + jnp.sum(skew_part * skew_part))
    identity = jnp.eye(pair_width, dtype=jnp.float32)
    rotator = (identity + skew_part) * factor
    for repeat in range(NS_STEPS):
        square = jnp.dot(rotator.T, rotator, precision=HIGH, preferred_element_type=jnp.float32)
        rotator = 1.5 * rotator - 0.5 * jnp.dot(rotator, square, precision=HIGH, preferred_element_type=jnp.float32)
    off_sq = jnp.sum(jnp.where(identity > 0.5, 0.0, gram_sum * gram_sum))
    diag_sq = jnp.sum(diag_vals * diag_vals)
    return (rotator, off_sq, diag_sq)

def reference(matrix, prior):
    row_count, col_count = matrix.shape
    blocks = N_BLK
    pair_width = col_count // blocks
    half_width = pair_width // 2
    frames = matrix.reshape(row_count, blocks, pair_width).transpose(1, 0, 2)
    earlier = prior.reshape(col_count, blocks, pair_width).transpose(1, 0, 2)
    frames = jnp.concatenate([frames, earlier], axis=1)

    def turn_pair(stacked):
        local_rows = stacked[:row_count]
        gram_sum = jnp.dot(local_rows.T, local_rows, precision=HIGH, preferred_element_type=jnp.float32)
        rotator, off_sq, diag_sq = rotation(gram_sum)
        return (jnp.dot(stacked, rotator, precision=HIGH, preferred_element_type=jnp.float32), off_sq, diag_sq)
    history = []
    for round_index in range(ROUNDS):
        frames, off_all, diag_all = lax.map(turn_pair, frames)
        history.append(jnp.sqrt(jnp.sum(off_all) / jnp.sum(diag_all)))
        top_turned = frames[:, :, :half_width]
        bottom_turned = frames[:, :, half_width:]
        new_top = jnp.concatenate([top_turned[:1], bottom_turned[:1], top_turned[1:blocks - 1]], axis=0)
        new_bottom = jnp.concatenate([bottom_turned[1:], top_turned[blocks - 1:]], axis=0)
        frames = jnp.concatenate([new_top, new_bottom], axis=2)
    result = frames.transpose(1, 0, 2).reshape(row_count + col_count, col_count)
    return (result[:row_count], result[row_count:], jnp.stack(history))
```

```python
import functools

import jax
import jax.numpy as jnp
from jax import lax
from jax.experimental import pallas as pl
from jax.experimental.pallas import tpu as pltpu
from jax.sharding import PartitionSpec as P

ROUNDS = 8
NS_STEPS = 8
WIDTH = 512
MESH = pl.DeviceIdType.MESH
BF16 = jnp.bfloat16
F32 = jnp.float32


def split(x):
    hi = x.astype(BF16)
    lo = (x - hi.astype(F32)).astype(BF16)
    return hi, lo


def nn(a, b):
    return lax.dot_general(a, b, (((1,), (0,)), ((), ())), preferred_element_type=F32)


def nt(a, b):
    return lax.dot_general(a, b, (((1,), (1,)), ((), ())), preferred_element_type=F32)


def polar_step(v):
    n = v.shape[0]
    hi, lo = split(v)
    both = jnp.concatenate([hi, lo], axis=1)
    twice = jnp.concatenate(
        [jnp.concatenate([hi, hi], axis=1), jnp.concatenate([lo, lo], axis=1)], axis=0
    )
    square = nt(both, twice)
    square = square[:, :n] + square[:, n:]
    shi, slo = split(square)
    lines = jnp.concatenate([both, both], axis=0)
    turned = nn(jnp.concatenate([shi, slo], axis=1), lines)
    return 1.5 * v - 0.5 * (turned[:, :n] + turned[:, n:])


def kernel(
    n_row, n_blk, c_mat, c_all, width,
    mat_ref, pri_ref, turned_ref, trans_ref, stats_ref,
    frame, outgo, halves, grams,
    send_sem, recv_sem, gsend_sem, grecv_sem,
):
    me_row = lax.axis_index("row")
    me = lax.axis_index("blk")
    half = frame.shape[3]
    pair = 2 * half
    has_up = me < n_blk - 1
    has_down = me > 0
    is_first = me == 0
    is_last = me == n_blk - 1

    barrier = pltpu.get_barrier_semaphore()
    for d in range(1, n_row):
        pl.semaphore_signal(
            barrier, inc=1, device_id=(lax.rem(me_row + d, n_row), me), device_id_type=MESH
        )

    @pl.when(has_up)
    def _():
        pl.semaphore_signal(barrier, inc=1, device_id=(me_row, me + 1), device_id_type=MESH)

    @pl.when(has_down)
    def _():
        pl.semaphore_signal(barrier, inc=1, device_id=(me_row, me - 1), device_id_type=MESH)

    peers = n_row - 1 + jnp.where(has_up, 1, 0) + jnp.where(has_down, 1, 0)
    pl.semaphore_wait(barrier, peers)

    up_src = jnp.where(is_first, 1, 0)

    def up_copy(par, c):
        return pltpu.make_async_remote_copy(
            src_ref=outgo.at[up_src, c], dst_ref=frame.at[par, 0, c],
            send_sem=send_sem.at[0, c], recv_sem=recv_sem.at[par, 0, c],
            device_id=(me_row, me + 1), device_id_type=MESH,
        )

    def down_copy(par, c):
        return pltpu.make_async_remote_copy(
            src_ref=outgo.at[1, c], dst_ref=frame.at[par, 1, c],
            send_sem=send_sem.at[1, c], recv_sem=recv_sem.at[par, 1, c],
            device_id=(me_row, me - 1), device_id_type=MESH,
        )

    def wait_sent(c):
        @pl.when(has_up)
        def _():
            up_copy(0, c).wait_send()

        @pl.when(has_down)
        def _():
            down_copy(0, c).wait_send()

    def wait_arrived(par, c):
        @pl.when(has_down)
        def _():
            up_copy(par, c).wait_recv()

        @pl.when(has_up)
        def _():
            down_copy(par, c).wait_recv()

    def load_halves(par, c):
        t = jnp.concatenate([frame[par, 0, c], frame[par, 1, c]], axis=0)
        hi, lo = split(t)
        stack = jnp.concatenate([hi, lo], axis=0)
        halves[c] = stack
        return stack

    def gram_copy(par, d):
        return pltpu.make_async_remote_copy(
            src_ref=grams.at[par, me_row], dst_ref=grams.at[par, me_row],
            send_sem=gsend_sem.at[d - 1], recv_sem=grecv_sem.at[par, d - 1],
            device_id=(lax.rem(me_row + d, n_row), me), device_id_type=MESH,
        )

    for c in range(c_all):
        if c < c_mat:
            t = mat_ref[pl.ds(c * width, width), :].T
        else:
            t = pri_ref[pl.ds((c - c_mat) * width, width), :].T
        frame[0, 0, c] = t[:half]
        frame[0, 1, c] = t[half:]

    rows = lax.broadcasted_iota(jnp.int32, (pair, pair), 0)
    cols = lax.broadcasted_iota(jnp.int32, (pair, pair), 1)
    eye = rows == cols
    lean = (rows - cols).astype(F32) / pair
    identity = eye.astype(F32)

    def one_round(k, carry):
        par = lax.rem(k, 2)
        nxt = 1 - par
        gram = jnp.zeros((pair, pair), F32)
        for c in range(c_mat):
            @pl.when(k > 0)
            def _():
                wait_arrived(par, c)

            stack = load_halves(par, c)
            p4 = nt(stack, stack)
            p2 = p4[:pair] + p4[pair:]
            gram = gram + (p2[:, :pair] + p2[:, pair:])
        grams[par, me_row] = gram
        for d in range(1, n_row):
            gram_copy(par, d).start()
        for d in range(1, n_row):
            gram_copy(par, d).wait()
        gram = grams[par, 0]
        for r in range(1, n_row):
            gram = gram + grams[par, r]

        gram_sq = gram * gram
        mean_diag = jnp.sum(jnp.where(eye, gram, 0.0)) / pair
        off_sq = jnp.sum(jnp.where(eye, 0.0, gram_sq))
        diag_sq = jnp.sum(jnp.where(eye, gram_sq, 0.0))
        lane = lax.broadcasted_iota(jnp.int32, (1, stats_ref.shape[1]), 1)
        stats_ref[pl.ds(k, 1), :] = jnp.where(
            lane == 0, off_sq, jnp.where(lane == 1, diag_sq, 0.0)
        )
        skew = gram * lean / mean_diag
        factor = lax.rsqrt(jnp.full((1, pair), 1.0, F32) + jnp.sum(skew * skew))
        v = (identity + skew) * factor
        v = lax.fori_loop(0, NS_STEPS, lambda s, x: polar_step(x), v)
        vhi, vlo = split(v)
        left = jnp.concatenate(
            [jnp.concatenate([vhi, vhi], axis=1), jnp.concatenate([vlo, vlo], axis=1)], axis=0
        )

        for c in range(c_all):
            @pl.when(k > 0)
            def _():
                wait_sent(c)
                if c >= c_mat:
                    wait_arrived(par, c)

            stack = halves[c] if c < c_mat else load_halves(par, c)
            both = nn(left, stack)
            rotated = both[:pair] + both[pair:]
            outgo[0, c] = rotated[:half]
            outgo[1, c] = rotated[half:]

            @pl.when(has_up)
            def _():
                up_copy(nxt, c).start()

            @pl.when(has_down)
            def _():
                down_copy(nxt, c).start()

            @pl.when(is_first)
            def _():
                frame[nxt, 0, c] = rotated[:half]

            @pl.when(is_last)
            def _():
                frame[nxt, 1, c] = rotated[:half]

        return carry

    lax.fori_loop(0, ROUNDS, one_round, 0)

    last = ROUNDS % 2
    for c in range(c_all):
        wait_arrived(last, c)
        wait_sent(c)
        t = jnp.concatenate([frame[last, 0, c], frame[last, 1, c]], axis=0).T
        if c < c_mat:
            turned_ref[pl.ds(c * width, width), :] = t
        else:
            trans_ref[pl.ds((c - c_mat) * width, width), :] = t


def body(matrix, prior):
    n_row = lax.axis_size("row")
    n_blk = lax.axis_size("blk")
    pair = matrix.shape[1]
    half = pair // 2
    width = min(WIDTH, matrix.shape[0], prior.shape[0])
    c_mat = matrix.shape[0] // width
    c_all = c_mat + prior.shape[0] // width
    vmem = pl.BlockSpec(memory_space=pltpu.VMEM)
    turned, trans, stats = pl.pallas_call(
        functools.partial(kernel, n_row, n_blk, c_mat, c_all, width),
        out_shape=(
            jax.ShapeDtypeStruct(matrix.shape, F32),
            jax.ShapeDtypeStruct(prior.shape, F32),
            jax.ShapeDtypeStruct((ROUNDS, 128), F32),
        ),
        in_specs=[vmem, vmem],
        out_specs=(vmem, vmem, vmem),
        scratch_shapes=[
            pltpu.VMEM((2, 2, c_all, half, width), F32),
            pltpu.VMEM((2, c_all, half, width), F32),
            pltpu.VMEM((c_all, 2 * pair, width), BF16),
            pltpu.VMEM((2, n_row, pair, pair), F32),
            pltpu.SemaphoreType.DMA((2, c_all)),
            pltpu.SemaphoreType.DMA((2, 2, c_all)),
            pltpu.SemaphoreType.DMA((max(n_row - 1, 1),)),
            pltpu.SemaphoreType.DMA((2, max(n_row - 1, 1))),
        ],
        compiler_params=pltpu.CompilerParams(
            collective_id=0, has_side_effects=True, vmem_limit_bytes=40 * 1024 * 1024
        ),
    )(matrix, prior)
    sums = lax.psum(stats[:, :2], "blk")
    return turned, trans, jnp.sqrt(sums[:, 0] / sums[:, 1])


def solution(mesh):
    return jax.shard_map(
        body,
        mesh=mesh,
        in_specs=(P("row", "blk"), P("row", "blk")),
        out_specs=(P("row", "blk"), P("row", "blk"), P()),
        check_vma=False,
    )
```

```python
import functools

import jax
import jax.numpy as jnp
from jax import lax
from jax.experimental import pallas as pl
from jax.experimental.pallas import tpu as pltpu
from jax.sharding import PartitionSpec as P

ROUNDS = 8
NS_STEPS = 8
WIDTH = 512
MESH = pl.DeviceIdType.MESH
BF16 = jnp.bfloat16
F32 = jnp.float32


def split(x):
    hi = x.astype(BF16)
    lo = (x - hi.astype(F32)).astype(BF16)
    return hi, lo


def nn(a, b):
    return lax.dot_general(a, b, (((1,), (0,)), ((), ())), preferred_element_type=F32)


def nt(a, b):
    return lax.dot_general(a, b, (((1,), (1,)), ((), ())), preferred_element_type=F32)


def polar_step(v):
    n = v.shape[0]
    hi, lo = split(v)
    both = jnp.concatenate([hi, lo], axis=1)
    twice = jnp.concatenate(
        [jnp.concatenate([hi, hi], axis=1), jnp.concatenate([lo, lo], axis=1)], axis=0
    )
    square = nt(both, twice)
    square = square[:, :n] + square[:, n:]
    shi, slo = split(square)
    lines = jnp.concatenate([both, both], axis=0)
    turned = nn(jnp.concatenate([shi, slo], axis=1), lines)
    return 1.5 * v - 0.5 * (turned[:, :n] + turned[:, n:])


def kernel(
    n_row, n_blk, c_mat, c_all, width, cores, side, doublings,
    mat_ref, pri_ref, turned_ref, trans_ref, stats_ref,
    frame, outgo, halves, grams, tallies,
    send_sem, recv_sem, gsend_sem, grecv_sem, ssend_sem, srecv_sem,
):
    me_row = lax.axis_index("row")
    me = lax.axis_index("blk")
    half = frame.shape[3]
    pair = 2 * half
    end = n_blk - 1
    final = ROUNDS - 1

    def place(p):
        chip = lax.div(p, cores)
        plane = lax.div(chip, side)
        spot = lax.rem(chip, side)
        spot = jnp.where(lax.rem(plane, 2) == 1, side - 1 - spot, spot)
        return (plane * side + spot) * cores + lax.rem(p, cores)

    mine = place(me)

    def above(p):
        return jnp.minimum(p + 1, end)

    def below(p):
        return jnp.maximum(p - 1, 0)

    def partner(j):
        step = 2 ** j
        return jnp.where(lax.rem(lax.div(me, step), 2) == 0, me + step, me - step)

    barrier = pltpu.get_barrier_semaphore()

    def greet(row, blk):
        pl.semaphore_signal(barrier, inc=1, device_id=(row, blk), device_id_type=MESH)

    peers = n_row - 1 + doublings
    for d in range(1, n_row):
        greet(lax.rem(me_row + d, n_row), me)
    for j in range(doublings):
        greet(me_row, partner(j))
    meets = [
        (mine < end, place(above(mine))), (mine > 0, place(below(mine))),
        (me < end, place(above(me))), (me > 0, place(below(me))),
        (mine < end, above(mine)), (mine > 0, below(mine)),
        ((me == end) & (mine != me), mine), ((mine == end) & (mine != me), mine),
    ]
    for on, blk in meets:
        @pl.when(on)
        def _():
            greet(me_row, blk)

        peers = peers + jnp.where(on, 1, 0)
    pl.semaphore_wait(barrier, peers)

    def slot_at(k):
        return jnp.where(k == 0, me, mine)

    def home_at(k, p):
        return jnp.where(k == final, p, place(p))

    def sends(k):
        s = slot_at(k)
        return (s < end) | (home_at(k, end) != me), s > 0

    def arrives(k):
        s = jnp.where(k == final + 1, me, mine)
        stays = jnp.where(k == 1, end == me, place(end) == me)
        return s > 0, (s < end) | jnp.logical_not(stays)

    def up_copy(k, par, c):
        s = slot_at(k)
        to = jnp.where(s == end, 1, 0)
        return pltpu.make_async_remote_copy(
            src_ref=outgo.at[jnp.where(s == 0, 1, 0), c], dst_ref=frame.at[par, to, c],
            send_sem=send_sem.at[0, c], recv_sem=recv_sem.at[par, to, c],
            device_id=(me_row, home_at(k, above(s))), device_id_type=MESH,
        )

    def down_copy(k, par, c):
        return pltpu.make_async_remote_copy(
            src_ref=outgo.at[1, c], dst_ref=frame.at[par, 1, c],
            send_sem=send_sem.at[1, c], recv_sem=recv_sem.at[par, 1, c],
            device_id=(me_row, home_at(k, below(slot_at(k)))), device_id_type=MESH,
        )

    def wait_sent(k, c):
        up_on, down_on = sends(k)

        @pl.when(up_on)
        def _():
            up_copy(k, 0, c).wait_send()

        @pl.when(down_on)
        def _():
            down_copy(k, 0, c).wait_send()

    def wait_arrived(k, par, c):
        for h, on in enumerate(arrives(k)):
            @pl.when(on)
            def _():
                pltpu.make_async_remote_copy(
                    src_ref=outgo.at[h, c], dst_ref=frame.at[par, h, c],
                    send_sem=send_sem.at[h, c], recv_sem=recv_sem.at[par, h, c],
                    device_id=(me_row, place(above(mine))), device_id_type=MESH,
                ).wait_recv()

    def load_halves(par, c):
        t = jnp.concatenate([frame[par, 0, c], frame[par, 1, c]], axis=0)
        hi, lo = split(t)
        stack = jnp.concatenate([hi, lo], axis=0)
        halves[c] = stack
        return stack

    def gram_copy(par, d):
        return pltpu.make_async_remote_copy(
            src_ref=grams.at[par, me_row], dst_ref=grams.at[par, me_row],
            send_sem=gsend_sem.at[d - 1], recv_sem=grecv_sem.at[par, d - 1],
            device_id=(lax.rem(me_row + d, n_row), me), device_id_type=MESH,
        )

    for c in range(c_all):
        if c < c_mat:
            t = mat_ref[pl.ds(c * width, width), :].T
        else:
            t = pri_ref[pl.ds((c - c_mat) * width, width), :].T
        frame[2, 0, c] = t[:half]
        frame[2, 1, c] = t[half:]

    rows = lax.broadcasted_iota(jnp.int32, (pair, pair), 0)
    cols = lax.broadcasted_iota(jnp.int32, (pair, pair), 1)
    eye = rows == cols
    lean = (rows - cols).astype(F32) / pair
    identity = eye.astype(F32)

    def one_round(k, carry):
        even = lax.rem(k, 2)
        par = jnp.where(k == 0, 2, even)
        nxt = jnp.where(k == final, 2, 1 - even)
        s = slot_at(k)
        up_on, down_on = sends(k)
        gram = jnp.zeros((pair, pair), F32)
        for c in range(c_mat):
            @pl.when(k > 0)
            def _():
                wait_arrived(k, par, c)

            stack = load_halves(par, c)
            p4 = nt(stack, stack)
            p2 = p4[:pair] + p4[pair:]
            gram = gram + (p2[:, :pair] + p2[:, pair:])
        grams[even, me_row] = gram
        for d in range(1, n_row):
            gram_copy(even, d).start()
        for d in range(1, n_row):
            gram_copy(even, d).wait()
        gram = grams[even, 0]
        for r in range(1, n_row):
            gram = gram + grams[even, r]

        gram_sq = gram * gram
        mean_diag = jnp.sum(jnp.where(eye, gram, 0.0)) / pair
        off_sq = jnp.sum(jnp.where(eye, 0.0, gram_sq))
        diag_sq = jnp.sum(jnp.where(eye, gram_sq, 0.0))
        lane = lax.broadcasted_iota(jnp.int32, (1, stats_ref.shape[1]), 1)
        tallies[0, pl.ds(k, 1), :] = jnp.where(
            lane == 0, off_sq, jnp.where(lane == 1, diag_sq, 0.0)
        )
        skew = gram * lean / mean_diag
        factor = lax.rsqrt(jnp.full((1, pair), 1.0, F32) + jnp.sum(skew * skew))
        v = (identity + skew) * factor
        v = lax.fori_loop(0, NS_STEPS, lambda s, x: polar_step(x), v)
        vhi, vlo = split(v)
        left = jnp.concatenate(
            [jnp.concatenate([vhi, vhi], axis=1), jnp.concatenate([vlo, vlo], axis=1)], axis=0
        )

        for c in range(c_all):
            @pl.when(k > 0)
            def _():
                wait_sent(k - 1, c)
                if c >= c_mat:
                    wait_arrived(k, par, c)

            stack = halves[c] if c < c_mat else load_halves(par, c)
            both = nn(left, stack)
            rotated = both[:pair] + both[pair:]
            outgo[0, c] = rotated[:half]
            outgo[1, c] = rotated[half:]

            @pl.when(up_on)
            def _():
                up_copy(k, nxt, c).start()

            @pl.when(down_on)
            def _():
                down_copy(k, nxt, c).start()

            @pl.when(s == 0)
            def _():
                frame[nxt, 0, c] = rotated[:half]

            @pl.when((s == end) & jnp.logical_not(up_on))
            def _():
                frame[nxt, 1, c] = rotated[:half]

        return carry

    lax.fori_loop(0, ROUNDS, one_round, 0)

    for j in range(doublings):
        copy = pltpu.make_async_remote_copy(
            src_ref=tallies.at[2 * j], dst_ref=tallies.at[2 * j + 1],
            send_sem=ssend_sem.at[j], recv_sem=srecv_sem.at[j],
            device_id=(me_row, partner(j)), device_id_type=MESH,
        )
        copy.start()
        copy.wait()
        tallies[2 * j + 2] = tallies[2 * j] + tallies[2 * j + 1]
    stats_ref[...] = tallies[2 * doublings]

    for c in range(c_all):
        wait_arrived(final + 1, 2, c)
        wait_sent(final, c)
        t = jnp.concatenate([frame[2, 0, c], frame[2, 1, c]], axis=0).T
        if c < c_mat:
            turned_ref[pl.ds(c * width, width), :] = t
        else:
            trans_ref[pl.ds((c - c_mat) * width, width), :] = t


def body(cores, side, matrix, prior):
    n_row = lax.axis_size("row")
    n_blk = lax.axis_size("blk")
    pair = matrix.shape[1]
    half = pair // 2
    width = min(WIDTH, matrix.shape[0], prior.shape[0])
    c_mat = matrix.shape[0] // width
    c_all = c_mat + prior.shape[0] // width
    doublings = n_blk.bit_length() - 1
    if 2**doublings != n_blk:
        doublings = 0
    vmem = pl.BlockSpec(memory_space=pltpu.VMEM)
    turned, trans, stats = pl.pallas_call(
        functools.partial(kernel, n_row, n_blk, c_mat, c_all, width, cores, side, doublings),
        out_shape=(
            jax.ShapeDtypeStruct(matrix.shape, F32),
            jax.ShapeDtypeStruct(prior.shape, F32),
            jax.ShapeDtypeStruct((ROUNDS, 128), F32),
        ),
        in_specs=[vmem, vmem],
        out_specs=(vmem, vmem, vmem),
        scratch_shapes=[
            pltpu.VMEM((3, 2, c_all, half, width), F32),
            pltpu.VMEM((2, c_all, half, width), F32),
            pltpu.VMEM((c_all, 2 * pair, width), BF16),
            pltpu.VMEM((2, n_row, pair, pair), F32),
            pltpu.VMEM((2 * doublings + 1, ROUNDS, 128), F32),
            pltpu.SemaphoreType.DMA((2, c_all)),
            pltpu.SemaphoreType.DMA((3, 2, c_all)),
            pltpu.SemaphoreType.DMA((max(n_row - 1, 1),)),
            pltpu.SemaphoreType.DMA((2, max(n_row - 1, 1))),
            pltpu.SemaphoreType.DMA((max(doublings, 1),)),
            pltpu.SemaphoreType.DMA((max(doublings, 1),)),
        ],
        compiler_params=pltpu.CompilerParams(
            collective_id=0, has_side_effects=True, vmem_limit_bytes=40 * 1024 * 1024
        ),
    )(matrix, prior)
    sums = stats[:, :2]
    if not doublings:
        sums = lax.psum(sums, "blk")
    return turned, trans, jnp.sqrt(sums[:, 0] / sums[:, 1])


def layout(mesh):
    coords = [tuple(getattr(d, "coords", None) or (0,)) for d in mesh.devices[0]]
    n = len(coords)
    cores = 1
    while cores < n and coords[cores] == coords[0]:
        cores += 1
    if n % cores:
        return 1, n
    chips = coords[::cores]
    side = 1
    while side < len(chips) and sum(abs(p - q) for p, q in zip(chips[side], chips[side - 1])) == 1:
        side += 1
    if len(chips) % side:
        side = len(chips)
    return cores, side


def solution(mesh):
    return jax.shard_map(
        functools.partial(body, *layout(mesh)),
        mesh=mesh,
        in_specs=(P("row", "blk"), P("row", "blk")),
        out_specs=(P("row", "blk"), P("row", "blk"), P()),
        check_vma=False,
    )
```

```python
import functools

import jax
import jax.numpy as jnp
from jax import lax
from jax.experimental import pallas as pl
from jax.experimental.pallas import tpu as pltpu
from jax.sharding import PartitionSpec as P

ROUNDS = 8
NS_STEPS = 8
WIDTH = 512
MESH = pl.DeviceIdType.MESH
BF16 = jnp.bfloat16
F32 = jnp.float32


def split(x):
    hi = x.astype(BF16)
    lo = (x - hi.astype(F32)).astype(BF16)
    return hi, lo


def nn(a, b):
    return lax.dot_general(a, b, (((1,), (0,)), ((), ())), preferred_element_type=F32)


def nt(a, b):
    return lax.dot_general(a, b, (((1,), (1,)), ((), ())), preferred_element_type=F32)


def polar_step(v):
    n = v.shape[0]
    hi, lo = split(v)
    both = jnp.concatenate([hi, lo], axis=1)
    twice = jnp.concatenate(
        [jnp.concatenate([hi, hi], axis=1), jnp.concatenate([lo, lo], axis=1)], axis=0
    )
    square = nt(both, twice)
    square = square[:, :n] + square[:, n:]
    shi, slo = split(square)
    lines = jnp.concatenate([both, both], axis=0)
    turned = nn(jnp.concatenate([shi, slo], axis=1), lines)
    return 1.5 * v - 0.5 * (turned[:, :n] + turned[:, n:])


def kernel(
    n_row, n_blk, c_mat, c_all, width, cores, side, doublings,
    mat_ref, pri_ref, turned_ref, trans_ref, stats_ref,
    frame, outgo, halves, grams, tallies,
    send_sem, recv_sem, gsend_sem, grecv_sem, ssend_sem, srecv_sem,
):
    me_row = lax.axis_index("row")
    me = lax.axis_index("blk")
    half = frame.shape[3]
    pair = 2 * half
    end = n_blk - 1
    final = ROUNDS - 1

    def place(p):
        chip = lax.div(p, cores)
        plane = lax.div(chip, side)
        spot = lax.rem(chip, side)
        spot = jnp.where(lax.rem(plane, 2) == 1, side - 1 - spot, spot)
        return (plane * side + spot) * cores + lax.rem(p, cores)

    mine = place(me)

    def above(p):
        return jnp.minimum(p + 1, end)

    def below(p):
        return jnp.maximum(p - 1, 0)

    def partner(j):
        step = 2 ** j
        return jnp.where(lax.rem(lax.div(me, step), 2) == 0, me + step, me - step)

    barrier = pltpu.get_barrier_semaphore()

    def greet(row, blk):
        pl.semaphore_signal(barrier, inc=1, device_id=(row, blk), device_id_type=MESH)

    peers = n_row - 1 + doublings
    for d in range(1, n_row):
        greet(lax.rem(me_row + d, n_row), me)
    for j in range(doublings):
        greet(me_row, partner(j))
    meets = [
        (mine < end, place(above(mine))), (mine > 0, place(below(mine))),
        (me < end, place(above(me))), (me > 0, place(below(me))),
        (mine < end, above(mine)), (mine > 0, below(mine)),
        ((me == end) & (mine != me), mine), ((mine == end) & (mine != me), mine),
    ]
    for on, blk in meets:
        @pl.when(on)
        def _():
            greet(me_row, blk)

        peers = peers + jnp.where(on, 1, 0)
    pl.semaphore_wait(barrier, peers)

    def slot_at(k):
        return jnp.where(k == 0, me, mine)

    def home_at(k, p):
        return jnp.where(k == final, p, place(p))

    def sends(k):
        s = slot_at(k)
        return (s < end) | (home_at(k, end) != me), s > 0

    def arrives(k):
        s = jnp.where(k == final + 1, me, mine)
        stays = jnp.where(k == 1, end == me, place(end) == me)
        return s > 0, (s < end) | jnp.logical_not(stays)

    def up_copy(k, par, c):
        s = slot_at(k)
        to = jnp.where(s == end, 1, 0)
        return pltpu.make_async_remote_copy(
            src_ref=outgo.at[jnp.where(s == 0, 1, 0), c], dst_ref=frame.at[par, to, c],
            send_sem=send_sem.at[0, c], recv_sem=recv_sem.at[par, to, c],
            device_id=(me_row, home_at(k, above(s))), device_id_type=MESH,
        )

    def down_copy(k, par, c):
        return pltpu.make_async_remote_copy(
            src_ref=outgo.at[1, c], dst_ref=frame.at[par, 1, c],
            send_sem=send_sem.at[1, c], recv_sem=recv_sem.at[par, 1, c],
            device_id=(me_row, home_at(k, below(slot_at(k)))), device_id_type=MESH,
        )

    def wait_sent(k, c):
        up_on, down_on = sends(k)

        @pl.when(up_on)
        def _():
            up_copy(k, 0, c).wait_send()

        @pl.when(down_on)
        def _():
            down_copy(k, 0, c).wait_send()

    def wait_arrived(k, par, c):
        for h, on in enumerate(arrives(k)):
            @pl.when(on)
            def _():
                pltpu.make_async_remote_copy(
                    src_ref=outgo.at[h, c], dst_ref=frame.at[par, h, c],
                    send_sem=send_sem.at[h, c], recv_sem=recv_sem.at[par, h, c],
                    device_id=(me_row, place(above(mine))), device_id_type=MESH,
                ).wait_recv()

    def load_halves(par, c):
        t = jnp.concatenate([frame[par, 0, c], frame[par, 1, c]], axis=0)
        hi, lo = split(t)
        stack = jnp.concatenate([hi, lo], axis=0)
        halves[c] = stack
        return stack

    def gram_copy(par, d):
        return pltpu.make_async_remote_copy(
            src_ref=grams.at[par, me_row], dst_ref=grams.at[par, me_row],
            send_sem=gsend_sem.at[d - 1], recv_sem=grecv_sem.at[par, d - 1],
            device_id=(lax.rem(me_row + d, n_row), me), device_id_type=MESH,
        )

    for c in range(c_all):
        if c < c_mat:
            t = mat_ref[pl.ds(c * width, width), :].T
        else:
            t = pri_ref[pl.ds((c - c_mat) * width, width), :].T
        frame[2, 0, c] = t[:half]
        frame[2, 1, c] = t[half:]

    rows = lax.broadcasted_iota(jnp.int32, (pair, pair), 0)
    cols = lax.broadcasted_iota(jnp.int32, (pair, pair), 1)
    eye = rows == cols
    lean = (rows - cols).astype(F32) / pair
    identity = eye.astype(F32)

    def one_round(k, carry):
        even = lax.rem(k, 2)
        par = jnp.where(k == 0, 2, even)
        nxt = jnp.where(k == final, 2, 1 - even)
        s = slot_at(k)
        up_on, down_on = sends(k)
        gram = jnp.zeros((pair, pair), F32)
        for c in range(c_mat):
            @pl.when(k > 0)
            def _():
                wait_arrived(k, par, c)

            stack = load_halves(par, c)
            p4 = nt(stack, stack)
            p2 = p4[:pair] + p4[pair:]
            gram = gram + (p2[:, :pair] + p2[:, pair:])
        grams[even, me_row] = gram
        for d in range(1, n_row):
            gram_copy(even, d).start()
        for d in range(1, n_row):
            gram_copy(even, d).wait()
        gram = grams[even, 0]
        for r in range(1, n_row):
            gram = gram + grams[even, r]

        gram_sq = gram * gram
        mean_diag = jnp.sum(jnp.where(eye, gram, 0.0)) / pair
        off_sq = jnp.sum(jnp.where(eye, 0.0, gram_sq))
        diag_sq = jnp.sum(jnp.where(eye, gram_sq, 0.0))
        lane = lax.broadcasted_iota(jnp.int32, (1, stats_ref.shape[1]), 1)
        tallies[0, pl.ds(k, 1), :] = jnp.where(
            lane == 0, off_sq, jnp.where(lane == 1, diag_sq, 0.0)
        )
        skew = gram * lean / mean_diag
        factor = lax.rsqrt(jnp.full((1, pair), 1.0, F32) + jnp.sum(skew * skew))
        v = (identity + skew) * factor
        v = lax.fori_loop(0, NS_STEPS, lambda s, x: polar_step(x), v)
        vhi, vlo = split(v)
        left = jnp.concatenate(
            [jnp.concatenate([vhi, vhi], axis=1), jnp.concatenate([vlo, vlo], axis=1)], axis=0
        )

        for c in range(c_all):
            @pl.when(k > 0)
            def _():
                wait_sent(k - 1, c)
                if c >= c_mat:
                    wait_arrived(k, par, c)

            stack = halves[c] if c < c_mat else load_halves(par, c)
            both = nn(left, stack)
            rotated = both[:pair] + both[pair:]
            outgo[0, c] = rotated[:half]
            outgo[1, c] = rotated[half:]

            @pl.when(up_on)
            def _():
                up_copy(k, nxt, c).start()

            @pl.when(down_on)
            def _():
                down_copy(k, nxt, c).start()

            @pl.when(s == 0)
            def _():
                frame[nxt, 0, c] = rotated[:half]

            @pl.when((s == end) & jnp.logical_not(up_on))
            def _():
                frame[nxt, 1, c] = rotated[:half]

        return carry

    lax.fori_loop(0, ROUNDS, one_round, 0)

    for j in range(doublings):
        copy = pltpu.make_async_remote_copy(
            src_ref=tallies.at[2 * j], dst_ref=tallies.at[2 * j + 1],
            send_sem=ssend_sem.at[j], recv_sem=srecv_sem.at[j],
            device_id=(me_row, partner(j)), device_id_type=MESH,
        )
        copy.start()
        copy.wait()
        tallies[2 * j + 2] = tallies[2 * j] + tallies[2 * j + 1]
    stats_ref[...] = tallies[2 * doublings]

    for c in range(c_all):
        wait_arrived(final + 1, 2, c)
        wait_sent(final, c)
        t = jnp.concatenate([frame[2, 0, c], frame[2, 1, c]], axis=0).T
        if c < c_mat:
            turned_ref[pl.ds(c * width, width), :] = t
        else:
            trans_ref[pl.ds((c - c_mat) * width, width), :] = t


def body(cores, side, matrix, prior):
    n_row = lax.axis_size("row")
    n_blk = lax.axis_size("blk")
    pair = matrix.shape[1]
    half = pair // 2
    width = min(WIDTH, matrix.shape[0], prior.shape[0])
    c_mat = matrix.shape[0] // width
    c_all = c_mat + prior.shape[0] // width
    doublings = n_blk.bit_length() - 1
    if 2**doublings != n_blk:
        doublings = 0
    vmem = pl.BlockSpec(memory_space=pltpu.VMEM)
    turned, trans, stats = pl.pallas_call(
        functools.partial(kernel, n_row, n_blk, c_mat, c_all, width, cores, side, doublings),
        out_shape=(
            jax.ShapeDtypeStruct(matrix.shape, F32),
            jax.ShapeDtypeStruct(prior.shape, F32),
            jax.ShapeDtypeStruct((ROUNDS, 128), F32),
        ),
        in_specs=[vmem, vmem],
        out_specs=(vmem, vmem, vmem),
        scratch_shapes=[
            pltpu.VMEM((3, 2, c_all, half, width), F32),
            pltpu.VMEM((2, c_all, half, width), F32),
            pltpu.VMEM((c_all, 2 * pair, width), BF16),
            pltpu.VMEM((2, n_row, pair, pair), F32),
            pltpu.VMEM((2 * doublings + 1, ROUNDS, 128), F32),
            pltpu.SemaphoreType.DMA((2, c_all)),
            pltpu.SemaphoreType.DMA((3, 2, c_all)),
            pltpu.SemaphoreType.DMA((max(n_row - 1, 1),)),
            pltpu.SemaphoreType.DMA((2, max(n_row - 1, 1))),
            pltpu.SemaphoreType.DMA((max(doublings, 1),)),
            pltpu.SemaphoreType.DMA((max(doublings, 1),)),
        ],
        compiler_params=pltpu.CompilerParams(
            collective_id=0, has_side_effects=True, vmem_limit_bytes=40 * 1024 * 1024
        ),
    )(matrix, prior)
    sums = stats[:, :2]
    if not doublings:
        sums = lax.psum(sums, "blk")
    return turned, trans, jnp.sqrt(sums[:, 0] / sums[:, 1])


def solution(mesh):
    return jax.shard_map(
        functools.partial(body, 1, mesh.shape["blk"]),
        mesh=mesh,
        in_specs=(P("row", "blk"), P("row", "blk")),
        out_specs=(P("row", "blk"), P("row", "blk"), P()),
        check_vma=False,
    )
```

```python
import functools

import jax
import jax.numpy as jnp
from jax import lax
from jax.experimental import pallas as pl
from jax.experimental.pallas import tpu as pltpu
from jax.sharding import PartitionSpec as P

ROUNDS = 8
NS_STEPS = 8
WIDTH = 256
MESH = pl.DeviceIdType.MESH
BF16 = jnp.bfloat16
F32 = jnp.float32


def split(x):
    hi = x.astype(BF16)
    lo = (x - hi.astype(F32)).astype(BF16)
    return hi, lo


def nn(a, b):
    return lax.dot_general(a, b, (((1,), (0,)), ((), ())), preferred_element_type=F32)


def nt(a, b):
    return lax.dot_general(a, b, (((1,), (1,)), ((), ())), preferred_element_type=F32)


def polar_step(v):
    n = v.shape[0]
    hi, lo = split(v)
    both = jnp.concatenate([hi, lo], axis=1)
    twice = jnp.concatenate(
        [jnp.concatenate([hi, hi], axis=1), jnp.concatenate([lo, lo], axis=1)], axis=0
    )
    square = nt(both, twice)
    square = square[:, :n] + square[:, n:]
    shi, slo = split(square)
    lines = jnp.concatenate([both, both], axis=0)
    turned = nn(jnp.concatenate([shi, slo], axis=1), lines)
    return 1.5 * v - 0.5 * (turned[:, :n] + turned[:, n:])


def kernel(
    n_row, n_blk, c_mat, c_all, width, cores, side, group,
    mat_ref, pri_ref, turned_ref, trans_ref, stats_ref,
    frame, outgo, halves, grams, tally, near, far,
    send_sem, recv_sem, gsend_sem, grecv_sem, ssend_sem, srecv_sem,
):
    me_row = lax.axis_index("row")
    me = lax.axis_index("blk")
    half = frame.shape[3]
    pair = 2 * half
    end = n_blk - 1
    final = ROUNDS - 1

    def place(p):
        chip = lax.div(p, cores)
        plane = lax.div(chip, side)
        spot = lax.rem(chip, side)
        spot = jnp.where(lax.rem(plane, 2) == 1, side - 1 - spot, spot)
        return (plane * side + spot) * cores + lax.rem(p, cores)

    mine = place(me)

    def above(p):
        return jnp.minimum(p + 1, end)

    def below(p):
        return jnp.maximum(p - 1, 0)

    groups = n_blk // group
    in_group = lax.rem(me, group)
    my_group = lax.div(me, group)

    def near_peer(d):
        return my_group * group + lax.rem(in_group + d, group)

    def far_peer(d):
        return lax.rem(my_group + d, groups) * group + in_group

    def near_copy(d):
        return pltpu.make_async_remote_copy(
            src_ref=near.at[in_group], dst_ref=near.at[in_group],
            send_sem=ssend_sem.at[d - 1], recv_sem=srecv_sem.at[d - 1],
            device_id=(me_row, near_peer(d)), device_id_type=MESH,
        )

    def far_copy(d):
        sem = group + d - 2
        return pltpu.make_async_remote_copy(
            src_ref=far.at[my_group], dst_ref=far.at[my_group],
            send_sem=ssend_sem.at[sem], recv_sem=srecv_sem.at[sem],
            device_id=(me_row, far_peer(d)), device_id_type=MESH,
        )

    barrier = pltpu.get_barrier_semaphore()

    def greet(row, blk):
        pl.semaphore_signal(barrier, inc=1, device_id=(row, blk), device_id_type=MESH)

    peers = n_row - 1 + group - 1 + groups - 1
    for d in range(1, n_row):
        greet(lax.rem(me_row + d, n_row), me)
    for d in range(1, group):
        greet(me_row, near_peer(d))
    for d in range(1, groups):
        greet(me_row, far_peer(d))
    meets = [
        (mine < end, place(above(mine))), (mine > 0, place(below(mine))),
        (me < end, place(above(me))), (me > 0, place(below(me))),
        (mine < end, above(mine)), (mine > 0, below(mine)),
        ((me == end) & (mine != me), mine), ((mine == end) & (mine != me), mine),
    ]
    for on, blk in meets:
        @pl.when(on)
        def _():
            greet(me_row, blk)

        peers = peers + jnp.where(on, 1, 0)
    pl.semaphore_wait(barrier, peers)

    def slot_at(k):
        return jnp.where(k == 0, me, mine)

    def home_at(k, p):
        return jnp.where(k == final, p, place(p))

    def sends(k):
        s = slot_at(k)
        return (s < end) | (home_at(k, end) != me), s > 0

    def arrives(k):
        s = jnp.where(k == final + 1, me, mine)
        stays = jnp.where(k == 1, end == me, place(end) == me)
        return s > 0, (s < end) | jnp.logical_not(stays)

    def up_copy(k, par, c):
        s = slot_at(k)
        to = jnp.where(s == end, 1, 0)
        return pltpu.make_async_remote_copy(
            src_ref=outgo.at[jnp.where(s == 0, 1, 0), c], dst_ref=frame.at[par, to, c],
            send_sem=send_sem.at[0, c], recv_sem=recv_sem.at[par, to, c],
            device_id=(me_row, home_at(k, above(s))), device_id_type=MESH,
        )

    def down_copy(k, par, c):
        return pltpu.make_async_remote_copy(
            src_ref=outgo.at[1, c], dst_ref=frame.at[par, 1, c],
            send_sem=send_sem.at[1, c], recv_sem=recv_sem.at[par, 1, c],
            device_id=(me_row, home_at(k, below(slot_at(k)))), device_id_type=MESH,
        )

    def wait_sent(k, c):
        up_on, down_on = sends(k)

        @pl.when(up_on)
        def _():
            up_copy(k, 0, c).wait_send()

        @pl.when(down_on)
        def _():
            down_copy(k, 0, c).wait_send()

    def wait_arrived(k, par, c):
        for h, on in enumerate(arrives(k)):
            @pl.when(on)
            def _():
                pltpu.make_async_remote_copy(
                    src_ref=outgo.at[h, c], dst_ref=frame.at[par, h, c],
                    send_sem=send_sem.at[h, c], recv_sem=recv_sem.at[par, h, c],
                    device_id=(me_row, place(above(mine))), device_id_type=MESH,
                ).wait_recv()

    def load_halves(par, c):
        t = jnp.concatenate([frame[par, 0, c], frame[par, 1, c]], axis=0)
        hi, lo = split(t)
        stack = jnp.concatenate([hi, lo], axis=0)
        halves[c] = stack
        return stack

    def gram_copy(par, d):
        return pltpu.make_async_remote_copy(
            src_ref=grams.at[par, me_row], dst_ref=grams.at[par, me_row],
            send_sem=gsend_sem.at[d - 1], recv_sem=grecv_sem.at[par, d - 1],
            device_id=(lax.rem(me_row + d, n_row), me), device_id_type=MESH,
        )

    def bring(ref, c, first):
        t = ref[pl.ds((c - first) * width, width), :].T
        frame[2, 0, c] = t[:half]
        frame[2, 1, c] = t[half:]

    for c in range(c_mat):
        bring(mat_ref, c, 0)

    rows = lax.broadcasted_iota(jnp.int32, (pair, pair), 0)
    cols = lax.broadcasted_iota(jnp.int32, (pair, pair), 1)
    eye = rows == cols
    lean = (rows - cols).astype(F32) / pair
    identity = eye.astype(F32)

    def one_round(k, carry):
        even = lax.rem(k, 2)
        par = jnp.where(k == 0, 2, even)
        nxt = jnp.where(k == final, 2, 1 - even)
        s = slot_at(k)
        up_on, down_on = sends(k)
        gram = jnp.zeros((pair, pair), F32)
        for c in range(c_mat):
            @pl.when(k > 0)
            def _():
                wait_arrived(k, par, c)

            stack = load_halves(par, c)
            p4 = nt(stack, stack)
            p2 = p4[:pair] + p4[pair:]
            gram = gram + (p2[:, :pair] + p2[:, pair:])
        grams[even, me_row] = gram
        for d in range(1, n_row):
            gram_copy(even, d).start()

        @pl.when(k == 0)
        def _():
            for c in range(c_mat, c_all):
                bring(pri_ref, c, c_mat)

        for d in range(1, n_row):
            gram_copy(even, d).wait()
        gram = grams[even, 0]
        for r in range(1, n_row):
            gram = gram + grams[even, r]

        gram_sq = gram * gram
        mean_diag = jnp.sum(jnp.where(eye, gram, 0.0)) / pair
        off_sq = jnp.sum(jnp.where(eye, 0.0, gram_sq))
        diag_sq = jnp.sum(jnp.where(eye, gram_sq, 0.0))
        lane = lax.broadcasted_iota(jnp.int32, (1, stats_ref.shape[1]), 1)
        tally[pl.ds(k, 1), :] = jnp.where(
            lane == 0, off_sq, jnp.where(lane == 1, diag_sq, 0.0)
        )

        @pl.when(k == final)
        def _():
            near[in_group] = tally[...]
            for d in range(1, group):
                near_copy(d).start()

        skew = gram * lean / mean_diag
        factor = lax.rsqrt(jnp.full((1, pair), 1.0, F32) + jnp.sum(skew * skew))
        v = (identity + skew) * factor
        v = lax.fori_loop(0, NS_STEPS, lambda s, x: polar_step(x), v)

        @pl.when(k == final)
        def _():
            for d in range(1, group):
                near_copy(d).wait()
            total = near[0]
            for r in range(1, group):
                total = total + near[r]
            far[my_group] = total
            for d in range(1, groups):
                far_copy(d).start()

        vhi, vlo = split(v)
        left = jnp.concatenate(
            [jnp.concatenate([vhi, vhi], axis=1), jnp.concatenate([vlo, vlo], axis=1)], axis=0
        )

        for c in range(c_all):
            @pl.when(k > 0)
            def _():
                wait_sent(k - 1, c)
                if c >= c_mat:
                    wait_arrived(k, par, c)

            stack = halves[c] if c < c_mat else load_halves(par, c)
            both = nn(left, stack)
            rotated = both[:pair] + both[pair:]
            outgo[0, c] = rotated[:half]
            outgo[1, c] = rotated[half:]

            @pl.when(up_on)
            def _():
                up_copy(k, nxt, c).start()

            @pl.when(down_on)
            def _():
                down_copy(k, nxt, c).start()

            @pl.when(s == 0)
            def _():
                frame[nxt, 0, c] = rotated[:half]

            @pl.when((s == end) & jnp.logical_not(up_on))
            def _():
                frame[nxt, 1, c] = rotated[:half]

        return carry

    lax.fori_loop(0, ROUNDS, one_round, 0)

    for d in range(1, groups):
        far_copy(d).wait()
    total = far[0]
    for r in range(1, groups):
        total = total + far[r]
    stats_ref[...] = total

    for c in range(c_all):
        wait_arrived(final + 1, 2, c)
        wait_sent(final, c)
        t = jnp.concatenate([frame[2, 0, c], frame[2, 1, c]], axis=0).T
        if c < c_mat:
            turned_ref[pl.ds(c * width, width), :] = t
        else:
            trans_ref[pl.ds((c - c_mat) * width, width), :] = t


def body(cores, side, matrix, prior):
    n_row = lax.axis_size("row")
    n_blk = lax.axis_size("blk")
    pair = matrix.shape[1]
    half = pair // 2
    width = min(WIDTH, matrix.shape[0], prior.shape[0])
    c_mat = matrix.shape[0] // width
    c_all = c_mat + prior.shape[0] // width
    group = max(g for g in range(1, n_blk + 1) if n_blk % g == 0 and g * g <= n_blk)
    sums_sent = max(group + n_blk // group - 2, 1)
    vmem = pl.BlockSpec(memory_space=pltpu.VMEM)
    turned, trans, stats = pl.pallas_call(
        functools.partial(kernel, n_row, n_blk, c_mat, c_all, width, cores, side, group),
        out_shape=(
            jax.ShapeDtypeStruct(matrix.shape, F32),
            jax.ShapeDtypeStruct(prior.shape, F32),
            jax.ShapeDtypeStruct((ROUNDS, 128), F32),
        ),
        in_specs=[vmem, vmem],
        out_specs=(vmem, vmem, vmem),
        scratch_shapes=[
            pltpu.VMEM((3, 2, c_all, half, width), F32),
            pltpu.VMEM((2, c_all, half, width), F32),
            pltpu.VMEM((c_all, 2 * pair, width), BF16),
            pltpu.VMEM((2, n_row, pair, pair), F32),
            pltpu.VMEM((ROUNDS, 128), F32),
            pltpu.VMEM((group, ROUNDS, 128), F32),
            pltpu.VMEM((n_blk // group, ROUNDS, 128), F32),
            pltpu.SemaphoreType.DMA((2, c_all)),
            pltpu.SemaphoreType.DMA((3, 2, c_all)),
            pltpu.SemaphoreType.DMA((max(n_row - 1, 1),)),
            pltpu.SemaphoreType.DMA((2, max(n_row - 1, 1))),
            pltpu.SemaphoreType.DMA((sums_sent,)),
            pltpu.SemaphoreType.DMA((sums_sent,)),
        ],
        compiler_params=pltpu.CompilerParams(
            collective_id=0, has_side_effects=True, vmem_limit_bytes=40 * 1024 * 1024
        ),
    )(matrix, prior)
    return turned, trans, jnp.sqrt(stats[:, 0] / stats[:, 1])


def solution(mesh):
    return jax.shard_map(
        functools.partial(body, 1, mesh.shape["blk"]),
        mesh=mesh,
        in_specs=(P("row", "blk"), P("row", "blk")),
        out_specs=(P("row", "blk"), P("row", "blk"), P()),
        check_vma=False,
    )
```
